32 devices in a mesh: groups: 2 (over x), row: 2 (over core), col: 8 (over z, y).
Axes of the slice: x: 2, y: 2, z: 4, core: 2. Of those that a mesh axis runs over, the one named last changes fastest.
Arguments:
- pair: bfloat16 [1280, 640, 128], P(('groups', 'col'), 'row'), parts along dimension 0, may hold values from -6 to 6
- token_mask: int32 [1280], P('groups'), parts along dimension 0, may hold values 0 or 1
- start_gain: float32 [128], replicated, may hold values from 0.25 to 1.75
- start_head_gain: float32 [128], replicated, may hold values from 0.25 to 1.75
- start_in: bfloat16 [128, 512], replicated, may hold values from -0.5 to 0.5
- start_out: bfloat16 [128, 128], replicated, may hold values from -0.5 to 0.5
- end_gain: float32 [128], replicated, may hold values from 0.25 to 1.75
- end_head_gain: float32 [128], replicated, may hold values from 0.25 to 1.75
- end_in: bfloat16 [128, 512], replicated, may hold values from -0.5 to 0.5
- end_out: bfloat16 [128, 128], replicated, may hold values from -0.5 to 0.5
- trans_gain: float32 [128], replicated, may hold values from 0.25 to 1.75
- trans_in: bfloat16 [128, 1024], replicated, may hold values from -0.5 to 0.5
- trans_out: bfloat16 [512, 128], replicated, may hold values from -0.25 to 0.25
Outputs:
- update_start: bfloat16 [1280, 640, 128], P(('groups', 'col'), 'row'), parts along dimension 0
- update_end: bfloat16 [1280, 640, 128], P(('groups', 'col'), 'row'), parts along dimension 0
- update_trans: bfloat16 [1280, 640, 128], P(('groups', 'col'), 'row'), parts along dimension 0
The draws below stay inside these ranges and needn't reach their ends.
There are 2 independent parts, one for each index of `groups`. The reference program is written for one: setup_inputs(seed, part) draws one part's arguments, and reference() takes and returns one part's arrays. A program takes and returns all parts, laid end to end along the dimension named above; an argument that names none is the same for every part. Nothing has to cross between parts.
Inputs may be any that keep to these rules, and one draw needn't show every extreme that they name: `token_mask`: 1 marks a valid token of the complex, 0 a padded one.
All inputs are finite; a program needn't handle non-finite values.
Results may differ from the reference program's by a relative error of at most 0.018.
Values may be sent and summed in bfloat16 or wider, within the bound.
A program may use at most 192 MiB of HBM per device.

```python
import jax
import jax.numpy as jnp
from jax import lax

N = 640
C = 128
HEADS = 4
TRANS = 512
N_ROW = 2
N_COL = 8


def touch_ends(result, key, low, high):
    longest = result.shape.index(max(result.shape))
    spots = []
    for shift in (0, 1):
        where = [jax.random.randint(jax.random.fold_in(key, axis), (), 0, length) for axis, length in enumerate(result.shape)]
        where[longest] = (where[longest] + shift) % result.shape[longest]
        spots.append(tuple(where))
    return result.at[spots[0]].set(low).at[spots[1]].set(high)


def block_levels(key, shape, split, least, top_value):
    def one(position, parts):
        draws = jax.random.uniform(jax.random.fold_in(jax.random.fold_in(key, 6), position), (parts,), jnp.float32, least / len(split), top_value / len(split))
        return jnp.repeat(jnp.exp(draws), shape[position] // parts).reshape((-1,) + (1,) * (len(shape) - position - 1))

    loudness = one(*split[0])
    for cut in split[1:]:
        loudness = loudness * one(*cut)
    return loudness


def normal_values(own_key, dims, deviation, limit, split=(), dtype=jnp.bfloat16):
    values = jax.random.normal(own_key, dims, jnp.float32) * deviation
    if len(split) > 0:
        values = block_levels(own_key, dims, split, -0.22, 0.18) * values
    return jnp.clip(values, min=-limit, max=limit).astype(dtype)


def setup_inputs(seed: int = 0, part: int = 0) -> dict:
    splits = jax.random.split(jax.random.key(seed), 14)
    own_keys = jax.random.split(jax.random.fold_in(splits[13], part), 14)
    return {
        "pair": normal_values(own_keys[0], (N, N, C), 1.0, 6.0, ((0, 8), (1, 2))),
        "token_mask": touch_ends((jax.random.randint(own_keys[1], (N,), 0, 8) < 7).astype(jnp.int32), jax.random.fold_in(own_keys[1], 1), 0, 1),
        "start_gain": jnp.clip(1.0 + 0.15 * jax.random.normal(splits[2], (C,), jnp.float32), 0.25, 1.75),
        "start_head_gain": jnp.clip(1.0 + 0.15 * jax.random.normal(splits[3], (C,), jnp.float32), 0.25, 1.75),
        "start_in": normal_values(splits[4], (C, 4 * C), C ** -0.5, 0.5),
        "start_out": normal_values(splits[5], (C, C), C ** -0.5, 0.5),
        "end_gain": jnp.clip(1.0 + 0.15 * jax.random.normal(splits[6], (C,), jnp.float32), 0.25, 1.75),
        "end_head_gain": jnp.clip(1.0 + 0.15 * jax.random.normal(splits[7], (C,), jnp.float32), 0.25, 1.75),
        "end_in": normal_values(splits[8], (C, 4 * C), C ** -0.5, 0.5),
        "end_out": normal_values(splits[9], (C, C), C ** -0.5, 0.5),
        "trans_gain": jnp.clip(1.0 + 0.15 * jax.random.normal(splits[10], (C,), jnp.float32), 0.25, 1.75),
        "trans_in": normal_values(splits[11], (C, 2 * TRANS), C ** -0.5, 0.5),
        "trans_out": normal_values(splits[12], (TRANS, C), TRANS ** -0.5, 0.25),
    }


EPSILON = 1e-05

def layer_norm(values, scales):
    average = lax.optimization_barrier(jnp.mean(values, axis=-1, keepdims=True))
    centered = values - average
    variance = lax.optimization_barrier(jnp.mean(centered * centered, axis=-1, keepdims=True))
    return centered * lax.rsqrt(variance + EPSILON) * scales.astype(jnp.float32)

def feature(values):
    return jax.nn.elu(values) + 1.0

def triangle(field, valid, ln_gain, head_gain, w_in, w_out, blocks):
    row_count, col_count, width = field.shape
    depth = width // HEADS
    stride = 16

    def one_block(operands):
        block, row_valid = operands
        normed = layer_norm(block, ln_gain).astype(jnp.bfloat16)
        project = jnp.dot(normed.reshape(-1, width), w_in, preferred_element_type=jnp.float32)
        project = project.reshape(stride, col_count, 4 * width)
        pair_valid = row_valid[:, None] * valid[None, :]
        queries = feature(project[..., :width]).astype(jnp.bfloat16).reshape(stride, col_count, HEADS, depth)
        key_feat = (feature(project[..., width:2 * width]) * pair_valid[..., None]).astype(jnp.bfloat16)
        key_feat = key_feat.reshape(stride, blocks, col_count // blocks, HEADS, depth)
        values = project[..., 2 * width:3 * width].astype(jnp.bfloat16)
        values = values.reshape(stride, blocks, col_count // blocks, HEADS, depth)
        gating = jax.nn.sigmoid(project[..., 3 * width:])
        partial_value = jnp.einsum('rbkhd,rbkhe->rbhde', key_feat.astype(jnp.float32), values.astype(jnp.float32))
        state = lax.optimization_barrier(jnp.sum(lax.optimization_barrier(partial_value.astype(jnp.bfloat16)).astype(jnp.float32), axis=1))
        key_part = lax.optimization_barrier(jnp.sum(key_feat.astype(jnp.float32), axis=2))
        totals = lax.optimization_barrier(jnp.sum(lax.optimization_barrier(key_part.astype(jnp.bfloat16)).astype(jnp.float32), axis=1))
        query_f = queries.astype(jnp.float32)
        numer = jnp.einsum('rkhd,rhde->rkhe', query_f, state)
        denom = jnp.maximum(jnp.einsum('rkhd,rhd->rkh', query_f, totals), 1.0)
        attended = (numer / denom[..., None]).reshape(stride, col_count, width)
        scaled = attended * lax.rsqrt(lax.optimization_barrier(jnp.mean(attended * attended, axis=-1, keepdims=True)) + EPSILON)
        scaled = (scaled * head_gain.astype(jnp.float32) * gating).astype(jnp.bfloat16)
        update = jnp.dot(scaled.reshape(-1, width), w_out, preferred_element_type=jnp.float32)
        return update.astype(jnp.bfloat16).reshape(stride, col_count, width)
    pieces = lax.map(one_block, (field.reshape(row_count // stride, stride, col_count, width), valid.reshape(row_count // stride, stride)))
    return pieces.reshape(row_count, col_count, width)

def reference(pair, token_mask, start_gain, start_head_gain, start_in, start_out, end_gain, end_head_gain, end_in, end_out, trans_gain, trans_in, trans_out):
    valid = token_mask.astype(jnp.float32)
    anchor = pair.astype(jnp.float32)
    update_start = triangle(anchor, valid, start_gain, start_head_gain, start_in, start_out, N_ROW)
    first_sum = anchor + update_start.astype(jnp.float32)
    flipped = triangle(jnp.transpose(first_sum, (1, 0, 2)), valid, end_gain, end_head_gain, end_in, end_out, N_COL)
    update_end = jnp.transpose(flipped, (1, 0, 2))
    second_sum = first_sum + update_end.astype(jnp.float32)
    width = pair.shape[2]
    hidden_width = trans_out.shape[0]
    stride = 16

    def transition(block):
        normed = layer_norm(block, trans_gain).astype(jnp.bfloat16)
        lifted = jnp.dot(normed.reshape(-1, width), trans_in, preferred_element_type=jnp.float32)
        hidden = (jax.nn.silu(lifted[:, :hidden_width]) * lifted[:, hidden_width:]).astype(jnp.bfloat16)
        return jnp.dot(hidden, trans_out, preferred_element_type=jnp.float32).astype(jnp.bfloat16)
    row_count = pair.shape[0]
    update_trans = lax.map(transition, second_sum.reshape(row_count // stride, stride, row_count, width))
    update_trans = update_trans.reshape(row_count, row_count, width)
    return (update_start, update_end, update_trans)
```

```python
import functools
import math

import jax
import jax.numpy as jnp
from jax import lax
from jax.experimental import pallas as pl
from jax.experimental.pallas import tpu as pltpu
from jax.sharding import PartitionSpec as P

HEADS = 4
EPSILON = 1e-05
F32 = jnp.float32
BF16 = jnp.bfloat16
CHUNKS = 2
VMEM_BYTES = 52 * 1024 * 1024


def layer_norm(values, scales):
    average = jnp.mean(values, axis=-1, keepdims=True)
    centered = values - average
    variance = jnp.mean(centered * centered, axis=-1, keepdims=True)
    return centered * lax.rsqrt(variance + EPSILON) * scales


def feature(values):
    return jnp.maximum(values + 1.0, jnp.exp(jnp.minimum(values, 0.0)))


def sigmoid(values):
    return 0.5 + 0.5 * jnp.tanh(0.5 * values)


def matmul(left, right):
    return jnp.dot(left, right, preferred_element_type=F32)


def same_head(width):
    depth = width // HEADS
    rows = lax.broadcasted_iota(jnp.int32, (width, width), 0) // depth
    cols = lax.broadcasted_iota(jnp.int32, (width, width), 1) // depth
    return rows == cols


def outer_compact(keys, values):
    width = keys.shape[-1]
    depth = width // HEADS
    full = lax.dot_general(keys, values, (((0,), (0,)), ((), ())), preferred_element_type=F32)
    head = lax.broadcasted_iota(jnp.int32, (depth, width), 1) // depth
    result = full[:depth]
    for h in range(1, HEADS):
        result = jnp.where(head == h, full[h * depth : (h + 1) * depth], result)
    return result


def expand(state, same):
    tiled = jnp.concatenate([state.astype(F32)] * HEADS, axis=0)
    return jnp.where(same, tiled, 0.0).astype(BF16)


def query_gate(w):
    width = w.shape[0]
    return jnp.concatenate([w[:, :width], w[:, 3 * width :]], axis=1)


def head_norm(numer, denom, gate, head_gain):
    attended = numer / jnp.maximum(denom, 1.0)
    scale = lax.rsqrt(jnp.mean(attended * attended, axis=-1, keepdims=True) + EPSILON)
    return (attended * scale * head_gain * sigmoid(gate)).astype(BF16)


def row_state_kernel(row_valid, pair, col_mask, gain, w, out):
    count, _, width = pair.shape
    depth = width // HEADS
    base = pl.program_id(0) * count
    w_kv = w[:, width : 3 * width]
    mask = col_mask[...]
    scales = gain[...]

    def one(i):
        normed = layer_norm(pair[i].astype(F32), scales).astype(BF16)
        project = matmul(normed, w_kv)
        keys = (feature(project[:, :width]) * mask).astype(BF16)
        values = project[:, width:].astype(BF16)
        valid = row_valid[base + i]
        out[i, 0:depth, :] = (outer_compact(keys, values) * valid).astype(BF16)
        total = jnp.sum(keys.astype(F32), axis=0, keepdims=True) * valid
        out[i, depth : depth + 16, :] = jnp.broadcast_to(total, (16, width)).astype(BF16)

    def body(step, carry):
        one(2 * step)
        one(2 * step + 1)
        return carry

    lax.fori_loop(0, count // 2, body, 0)


def start_kernel(pair, state, gain, head_gain, w, w_out, end_gain, *rest):
    update, normed_end = rest[-2:]
    count, _, width = pair.shape
    depth = width // HEADS
    same = same_head(width)
    ones = same.astype(F32).astype(BF16)
    w_qg = query_gate(w[...])

    def one(i):
        field = pair[i].astype(F32)
        normed = layer_norm(field, gain[...]).astype(BF16)
        project = matmul(normed, w_qg)
        queries = feature(project[:, :width]).astype(BF16)
        totals = state[i, depth : depth + 16, :].astype(F32)[0:1]
        numer = matmul(queries, expand(state[i, 0:depth, :], same))
        denom = matmul((queries.astype(F32) * totals).astype(BF16), ones)
        scaled = head_norm(numer, denom, project[:, width:], head_gain[...])
        result = matmul(scaled, w_out[...]).astype(BF16)
        update[i] = result
        normed_end[i] = layer_norm(field + result.astype(F32), end_gain[...]).astype(BF16)

    def body(step, carry):
        one(2 * step)
        one(2 * step + 1)
        return carry

    lax.fori_loop(0, count // 2, body, 0)


def columns_first(normed, scratch):
    rows, count, width = normed.shape
    scratch[...] = normed[...].astype(F32).reshape(rows * count, width)
    return jnp.concatenate(
        [scratch[pl.ds(j, rows, stride=count), :] for j in range(count)], axis=0
    ).astype(BF16)


def column_state_kernel(first, col_valid, normed, row_mask, w, out, scratch):
    rows, count, width = normed.shape
    depth = width // HEADS
    base = first + pl.program_id(0) * count
    project = matmul(columns_first(normed, scratch), w[:, width : 3 * width])
    keys = feature(project[:, :width]).reshape(count, rows, width) * row_mask[...][None]
    keys = keys.astype(BF16)
    values = project[:, width:].reshape(count, rows, width).astype(BF16)
    totals = []
    for j in range(count):
        valid = col_valid[base + j]
        out[0, j * depth : (j + 1) * depth, :] = (
            outer_compact(keys[j], values[j]) * valid
        ).astype(BF16)
        totals.append(jnp.sum(keys[j].astype(F32), axis=0, keepdims=True) * valid)
    out[0, count * depth : count * (depth + 1), :] = jnp.concatenate(totals, axis=0).astype(BF16)
    left = out.shape[1] - count * (depth + 1)
    if left:
        out[0, count * (depth + 1) :, :] = jnp.zeros((left, width), BF16)


def end_kernel(
    normed, pair, update_start, state, head_gain, w, w_out, trans_gain, trans_in, trans_out, *rest
):
    update_end, update_trans, scratch, turned = rest[-4:]
    rows, count, width = normed.shape
    depth = width // HEADS
    hidden = trans_out.shape[0]
    same = same_head(width)
    ones = same.astype(F32).astype(BF16)
    project = matmul(columns_first(normed, scratch), query_gate(w[...]))
    queries = feature(project[:, :width]).reshape(count, rows, width).astype(BF16)
    totals = state[0, count * depth : count * (depth + 1), :].astype(F32)
    numer, weighted = [], []
    for j in range(count):
        numer.append(matmul(queries[j], expand(state[0, j * depth : (j + 1) * depth, :], same)))
        weighted.append(queries[j].astype(F32) * totals[j : j + 1])
    denom = matmul(jnp.concatenate(weighted, axis=0).astype(BF16), ones)
    scaled = head_norm(
        jnp.concatenate(numer, axis=0), denom, project[:, width:], head_gain[...]
    )
    result = matmul(scaled, w_out[...])
    for j in range(count):
        turned[pl.ds(j, rows, stride=count), :] = result[j * rows : (j + 1) * rows]
    stride = math.gcd(rows, 16)

    def body(step, carry):
        at = pl.ds(step * stride, stride)
        flat = pl.ds(pl.multiple_of(step * stride * count, stride * count), stride * count)
        ended = turned[flat, :].astype(BF16)
        update_end[at] = ended.reshape(stride, count, width)
        field = pair[at].astype(F32) + update_start[at].astype(F32)
        field = field.reshape(stride * count, width) + ended.astype(F32)
        y = layer_norm(field, trans_gain[...]).astype(BF16)
        lifted = matmul(y, trans_in[...])
        gate = 0.5 * lifted[:, :hidden]
        h = ((gate + gate * jnp.tanh(gate)) * lifted[:, hidden:]).astype(BF16)
        moved = matmul(h, trans_out[...]).astype(BF16)
        update_trans[at] = moved.reshape(stride, count, width)
        return carry

    lax.fori_loop(0, rows // stride, body, 0)


def exchange_sum(values, size, bits):
    me = lax.axis_index("col")
    for bit in bits:
        half = values.shape[0] // 2
        mine = (me >> bit) & 1
        pairs = [(d, d ^ (1 << bit)) for d in range(size)]
        sent = lax.dynamic_slice_in_dim(values, (1 - mine) * half, half)
        kept = lax.dynamic_slice_in_dim(values, mine * half, half)
        got = lax.ppermute(sent, "col", pairs)
        values = (kept.astype(F32) + got.astype(F32)).astype(BF16)
    for bit in reversed(bits):
        mine = (me >> bit) & 1
        pairs = [(d, d ^ (1 << bit)) for d in range(size)]
        got = lax.ppermute(values, "col", pairs)
        values = jnp.where(
            mine == 1,
            jnp.concatenate([got, values], axis=0),
            jnp.concatenate([values, got], axis=0),
        )
    return values


def params():
    return pltpu.CompilerParams(vmem_limit_bytes=VMEM_BYTES, dimension_semantics=("arbitrary",))


def cost(flops):
    return pl.CostEstimate(flops=int(flops), bytes_accessed=1 << 20, transcendentals=0)


def shards(
    size,
    pair,
    token_mask,
    start_gain,
    start_head_gain,
    start_in,
    start_out,
    end_gain,
    end_head_gain,
    end_in,
    end_out,
    trans_gain,
    trans_in,
    trans_out,
):
    rows, cols, width = pair.shape
    depth = width // HEADS
    valid = token_mask.astype(F32)
    row_valid = lax.dynamic_slice_in_dim(valid, lax.axis_index("col") * rows, rows)
    col_valid = lax.dynamic_slice_in_dim(valid, lax.axis_index("row") * cols, cols)
    row_mask = jnp.broadcast_to(row_valid[:, None], (rows, width))
    col_mask = jnp.broadcast_to(col_valid[:, None], (cols, width))
    gains = [
        g.reshape(1, width) for g in (start_gain, start_head_gain, end_gain, end_head_gain, trans_gain)
    ]
    start_gain, start_head_gain, end_gain, end_head_gain, trans_gain = gains
    smem = pl.BlockSpec(memory_space=pltpu.SMEM)
    anywhere = pl.BlockSpec(memory_space=pl.ANY)

    def whole(array):
        return pl.BlockSpec(array.shape, lambda g: (0,) * array.ndim)

    group = math.gcd(rows, 8)
    packed = depth + 16
    row_state = pl.pallas_call(
        row_state_kernel,
        grid=(rows // group,),
        in_specs=[
            smem,
            pl.BlockSpec((group, cols, width), lambda g: (g, 0, 0)),
            whole(col_mask),
            whole(start_gain),
            whole(start_in),
        ],
        out_specs=pl.BlockSpec((group, packed, width), lambda g: (g, 0, 0)),
        out_shape=jax.ShapeDtypeStruct((rows, packed, width), BF16),
        compiler_params=params(),
        cost_estimate=cost(2e10),
        name="row_state",
    )(row_valid, pair, col_mask, start_gain, start_in)
    row_state = lax.psum(row_state, "row")

    part = cols // CHUNKS
    tile = 16
    tiles = part // tile
    block = tile * (depth + 1)
    while block % 16 or (tiles * block) % (16 * size):
        block += 16
    bits = list(range(size.bit_length() - 1))
    full = jax.ShapeDtypeStruct(pair.shape, BF16)

    update_start = None
    normed_parts, column_states = [], []
    for chunk in range(CHUNKS):
        extra = [] if update_start is None else [update_start]
        pair_block = pl.BlockSpec((group, part, width), lambda g, c=chunk: (g, c, 0))
        update_start, normed = pl.pallas_call(
            start_kernel,
            grid=(rows // group,),
            in_specs=[
                pair_block,
                pl.BlockSpec((group, packed, width), lambda g: (g, 0, 0)),
                whole(start_gain),
                whole(start_head_gain),
                whole(start_in),
                whole(start_out),
                whole(end_gain),
            ]
            + [anywhere] * len(extra),
            out_specs=[pair_block, pl.BlockSpec((group, part, width), lambda g: (g, 0, 0))],
            out_shape=[full, jax.ShapeDtypeStruct((rows, part, width), BF16)],
            input_output_aliases={7: 0} if extra else {},
            compiler_params=params(),
            cost_estimate=cost(2e10),
            name="start_finish",
        )(pair, row_state, start_gain, start_head_gain, start_in, start_out, end_gain, *extra)
        normed_parts.append(normed)
        state = pl.pallas_call(
            functools.partial(column_state_kernel, chunk * part),
            grid=(tiles,),
            in_specs=[
                smem,
                pl.BlockSpec((rows, tile, width), lambda g: (0, g, 0)),
                whole(row_mask),
                whole(end_in),
            ],
            out_specs=pl.BlockSpec((1, block, width), lambda g: (g, 0, 0)),
            out_shape=jax.ShapeDtypeStruct((tiles, block, width), BF16),
            scratch_shapes=[pltpu.VMEM((rows * tile, width), F32)],
            compiler_params=params(),
            cost_estimate=cost(1e10),
            name="column_state",
        )(col_valid, normed, row_mask, end_in)
        order = bits if chunk % 2 == 0 else bits[1:] + bits[:1]
        state = exchange_sum(state.reshape(tiles * block, width), size, order)
        column_states.append(state.reshape(tiles, block, width))

    outs = []
    for chunk in range(CHUNKS):
        pair_block = pl.BlockSpec(
            (rows, tile, width), lambda g, c=chunk: (0, c * tiles + g, 0)
        )
        outs = pl.pallas_call(
            end_kernel,
            grid=(tiles,),
            in_specs=[
                pl.BlockSpec((rows, tile, width), lambda g: (0, g, 0)),
                pair_block,
                pair_block,
                pl.BlockSpec((1, block, width), lambda g: (g, 0, 0)),
                whole(end_head_gain),
                whole(end_in),
                whole(end_out),
                whole(trans_gain),
                whole(trans_in),
                whole(trans_out),
            ]
            + [anywhere] * len(outs),
            out_specs=[pair_block, pair_block],
            out_shape=[full, full],
            scratch_shapes=[pltpu.VMEM((rows * tile, width), F32)] * 2,
            input_output_aliases={10: 0, 11: 1} if outs else {},
            compiler_params=params(),
            cost_estimate=cost(5e10),
            name="end_finish",
        )(
            normed_parts[chunk],
            pair,
            update_start,
            column_states[chunk],
            end_head_gain,
            end_in,
            end_out,
            trans_gain,
            trans_in,
            trans_out,
            *outs,
        )
    return (update_start, outs[0], outs[1])


def solution(mesh):
    field = P(("groups", "col"), "row", None)
    in_specs = (field, P("groups")) + (P(),) * 11
    return jax.shard_map(
        functools.partial(shards, mesh.shape["col"]),
        mesh=mesh,
        in_specs=in_specs,
        out_specs=(field, field, field),
        check_vma=False,
    )
```

```python
import functools
import math

import jax
import jax.numpy as jnp
from jax import lax
from jax.experimental import pallas as pl
from jax.experimental.pallas import tpu as pltpu
from jax.sharding import PartitionSpec as P

HEADS = 4
EPSILON = 1e-05
F32 = jnp.float32
BF16 = jnp.bfloat16
CHUNKS = 4
VMEM_BYTES = 52 * 1024 * 1024


def mean_matrix(width):
    return jnp.full((width, width), 1.0 / width, BF16)


def center_matrix(width, copies):
    rows = lax.broadcasted_iota(jnp.int32, (width, width), 0)
    cols = lax.broadcasted_iota(jnp.int32, (width, width), 1)
    once = jnp.where(rows == cols, 1.0 - 1.0 / width, -1.0 / width)
    return jnp.concatenate([once] * copies, axis=0).astype(BF16)


def layer_norm(parts, scales):
    width = parts[0].shape[-1]
    joined = parts[0] if len(parts) == 1 else jnp.concatenate(parts, axis=1)
    centered = matmul(joined, center_matrix(width, len(parts)))
    variance = matmul((centered * centered).astype(BF16), mean_matrix(width))
    return (centered * lax.rsqrt(variance + EPSILON) * scales).astype(BF16)


def feature(values):
    return jnp.maximum(values + 1.0, jnp.exp(jnp.minimum(values, 0.0)))


def sigmoid(values):
    return 0.5 + 0.5 * jnp.tanh(0.5 * values)


def matmul(left, right):
    return jnp.dot(left, right, preferred_element_type=F32)


def same_head(width):
    depth = width // HEADS
    rows = lax.broadcasted_iota(jnp.int32, (width, width), 0) // depth
    cols = lax.broadcasted_iota(jnp.int32, (width, width), 1) // depth
    return rows == cols


def outer_compact(keys, values):
    width = keys.shape[-1]
    depth = width // HEADS
    full = lax.dot_general(keys, values, (((0,), (0,)), ((), ())), preferred_element_type=F32)
    head = lax.broadcasted_iota(jnp.int32, (depth, width), 1) // depth
    result = full[:depth]
    for h in range(1, HEADS):
        result = jnp.where(head == h, full[h * depth : (h + 1) * depth], result)
    return result


def expand(state, same):
    tiled = jnp.concatenate([state.astype(F32)] * HEADS, axis=0)
    return jnp.where(same, tiled, 0.0).astype(BF16)


def query_gate(w):
    width = w.shape[0]
    return jnp.concatenate([w[:, :width], w[:, 3 * width :]], axis=1)


def head_norm(numer, denom, gate, head_gain):
    attended = numer / jnp.maximum(denom, 1.0)
    square = matmul((attended * attended).astype(BF16), mean_matrix(numer.shape[-1]))
    scale = lax.rsqrt(square + EPSILON)
    return (attended * scale * head_gain * sigmoid(gate)).astype(BF16)


def row_state_kernel(row_valid, pair, col_mask, gain, w, out):
    count, cols, width = pair.shape
    depth = width // HEADS
    base = pl.program_id(0) * count
    normed = layer_norm([pair[...].reshape(count * cols, width)], gain[...])
    project = matmul(normed, w[:, width : 3 * width])
    keys = feature(project[:, :width]).reshape(count, cols, width) * col_mask[...][None]
    keys = keys.astype(BF16)
    values = project[:, width:].reshape(count, cols, width).astype(BF16)
    for i in range(count):
        valid = row_valid[base + i]
        out[i, 0:depth, :] = (outer_compact(keys[i], values[i]) * valid).astype(BF16)
        total = jnp.sum(keys[i].astype(F32), axis=0, keepdims=True) * valid
        out[i, depth : depth + 16, :] = jnp.broadcast_to(total, (16, width)).astype(BF16)


def start_kernel(row_size, pair, *rest):
    states, rest = rest[:row_size], rest[row_size:]
    gain, head_gain, w, w_out, end_gain = rest[:5]
    update, normed_end = rest[-2:]
    count, cols, width = pair.shape
    depth = width // HEADS
    same = same_head(width)
    ones = same.astype(F32).astype(BF16)
    field = pair[...].reshape(count * cols, width)
    project = matmul(layer_norm([field], gain[...]), query_gate(w[...]))
    queries = feature(project[:, :width]).reshape(count, cols, width).astype(BF16)
    numer, weighted = [], []
    for i in range(count):
        state = sum(s[i, 0:depth, :].astype(F32) for s in states)
        totals = sum(s[i, depth : depth + 16, :].astype(F32) for s in states)
        numer.append(matmul(queries[i], expand(state, same)))
        weighted.append(queries[i].astype(F32) * totals[0:1])
    denom = matmul(jnp.concatenate(weighted, axis=0).astype(BF16), ones)
    scaled = head_norm(
        jnp.concatenate(numer, axis=0), denom, project[:, width:], head_gain[...]
    )
    result = matmul(scaled, w_out[...]).astype(BF16)
    update[...] = result.reshape(count, cols, width)
    normed_end[...] = layer_norm([field, result], end_gain[...]).reshape(count, cols, width)


def columns_first(normed, scratch):
    rows, count, width = normed.shape
    scratch[...] = normed[...].astype(F32).reshape(rows * count, width)
    return jnp.concatenate(
        [scratch[pl.ds(j, rows, stride=count), :] for j in range(count)], axis=0
    ).astype(BF16)


def column_state_kernel(first, col_valid, normed, row_mask, w, out, scratch):
    rows, count, width = normed.shape
    depth = width // HEADS
    base = first + pl.program_id(0) * count
    project = matmul(columns_first(normed, scratch), w[:, width : 3 * width])
    keys = feature(project[:, :width]).reshape(count, rows, width) * row_mask[...][None]
    keys = keys.astype(BF16)
    values = project[:, width:].reshape(count, rows, width).astype(BF16)
    totals = []
    for j in range(count):
        valid = col_valid[base + j]
        out[0, j * depth : (j + 1) * depth, :] = (
            outer_compact(keys[j], values[j]) * valid
        ).astype(BF16)
        totals.append(jnp.sum(keys[j].astype(F32), axis=0, keepdims=True) * valid)
    out[0, count * depth : count * (depth + 1), :] = jnp.concatenate(totals, axis=0).astype(BF16)


def end_kernel(
    normed, pair, update_start, state, head_gain, w, w_out, trans_gain, trans_in, trans_out, *rest
):
    update_end, update_trans, scratch, turned = rest[-4:]
    rows, count, width = normed.shape
    depth = width // HEADS
    hidden = trans_out.shape[0]
    same = same_head(width)
    ones = same.astype(F32).astype(BF16)
    project = matmul(columns_first(normed, scratch), query_gate(w[...]))
    queries = feature(project[:, :width]).reshape(count, rows, width).astype(BF16)
    totals = state[0, count * depth : count * (depth + 1), :].astype(F32)
    numer, weighted = [], []
    for j in range(count):
        numer.append(matmul(queries[j], expand(state[0, j * depth : (j + 1) * depth, :], same)))
        weighted.append(queries[j].astype(F32) * totals[j : j + 1])
    denom = matmul(jnp.concatenate(weighted, axis=0).astype(BF16), ones)
    scaled = head_norm(
        jnp.concatenate(numer, axis=0), denom, project[:, width:], head_gain[...]
    )
    result = matmul(scaled, w_out[...])
    for j in range(count):
        turned[pl.ds(j, rows, stride=count), :] = result[j * rows : (j + 1) * rows]
    stride = math.gcd(rows, 16)

    def body(step, carry):
        at = pl.ds(step * stride, stride)
        flat = pl.ds(pl.multiple_of(step * stride * count, stride * count), stride * count)
        ended = turned[flat, :].astype(BF16)
        update_end[at] = ended.reshape(stride, count, width)
        parts = [part[at].reshape(stride * count, width) for part in (pair, update_start)]
        y = layer_norm(parts + [ended], trans_gain[...])
        lifted = matmul(y, trans_in[...])
        gate = 0.5 * lifted[:, :hidden]
        h = ((gate + gate * jnp.tanh(gate)) * lifted[:, hidden:]).astype(BF16)
        moved = matmul(h, trans_out[...]).astype(BF16)
        update_trans[at] = moved.reshape(stride, count, width)
        return carry

    lax.fori_loop(0, rows // stride, body, 0, unroll=True)


def exchange_sum(values, size, bits, done):
    me = lax.axis_index("col")
    for bit in bits:
        yield values
        half = values.shape[0] // 2
        mine = (me >> bit) & 1
        pairs = [(d, d ^ (1 << bit)) for d in range(size)]
        sent = lax.dynamic_slice_in_dim(values, (1 - mine) * half, half)
        kept = lax.dynamic_slice_in_dim(values, mine * half, half)
        got = lax.ppermute(sent, "col", pairs)
        values = (kept.astype(F32) + got.astype(F32)).astype(BF16)
    for bit in reversed(bits):
        yield values
        mine = (me >> bit) & 1
        pairs = [(d, d ^ (1 << bit)) for d in range(size)]
        got = lax.ppermute(values, "col", pairs)
        values = jnp.where(
            mine == 1,
            jnp.concatenate([got, values], axis=0),
            jnp.concatenate([values, got], axis=0),
        )
    done.append(values)


def params():
    return pltpu.CompilerParams(vmem_limit_bytes=VMEM_BYTES, dimension_semantics=("arbitrary",))


def cost(flops):
    return pl.CostEstimate(flops=int(flops), bytes_accessed=1 << 20, transcendentals=0)


def shards(
    size,
    row_size,
    pair,
    token_mask,
    start_gain,
    start_head_gain,
    start_in,
    start_out,
    end_gain,
    end_head_gain,
    end_in,
    end_out,
    trans_gain,
    trans_in,
    trans_out,
):
    rows, cols, width = pair.shape
    depth = width // HEADS
    valid = token_mask.astype(F32)
    row_valid = lax.dynamic_slice_in_dim(valid, lax.axis_index("col") * rows, rows)
    col_valid = lax.dynamic_slice_in_dim(valid, lax.axis_index("row") * cols, cols)
    row_mask = jnp.broadcast_to(row_valid[:, None], (rows, width))
    col_mask = jnp.broadcast_to(col_valid[:, None], (cols, width))
    gains = [
        g.reshape(1, width) for g in (start_gain, start_head_gain, end_gain, end_head_gain, trans_gain)
    ]
    start_gain, start_head_gain, end_gain, end_head_gain, trans_gain = gains
    smem = pl.BlockSpec(memory_space=pltpu.SMEM)
    anywhere = pl.BlockSpec(memory_space=pl.ANY)

    def whole(array):
        return pl.BlockSpec(array.shape, lambda g: (0,) * array.ndim)

    group = math.gcd(rows, 8)
    packed = depth + 16
    row_state = pl.pallas_call(
        row_state_kernel,
        grid=(rows // group,),
        in_specs=[
            smem,
            pl.BlockSpec((group, cols, width), lambda g: (g, 0, 0)),
            whole(col_mask),
            whole(start_gain),
            whole(start_in),
        ],
        out_specs=pl.BlockSpec((group, packed, width), lambda g: (g, 0, 0)),
        out_shape=jax.ShapeDtypeStruct((rows, packed, width), BF16),
        compiler_params=params(),
        cost_estimate=cost(2e10),
        name="row_state",
    )(row_valid, pair, col_mask, start_gain, start_in)
    row_states = [row_state] + [
        lax.ppermute(row_state, "row", [(d, (d + k) % row_size) for d in range(row_size)])
        for k in range(1, row_size)
    ]

    tile = 16
    chunks = math.gcd(cols // tile, CHUNKS)
    part = cols // chunks
    tiles = part // tile
    block = tile * (depth + 1)
    pad = -(tiles * block) % (16 * size)
    bits = list(range(size.bit_length() - 1))
    full = jax.ShapeDtypeStruct(pair.shape, BF16)
    flying = []

    def advance(small):
        for steps in list(flying):
            ready = next(steps, None)
            if ready is None:
                flying.remove(steps)
            else:
                small, _ = lax.optimization_barrier((small, ready))
        return small

    group = math.gcd(rows, 16)
    update_start = None
    normed_parts, column_states = [], []
    for chunk in range(chunks):
        extra = [] if update_start is None else [update_start]
        pair_block = pl.BlockSpec((group, part, width), lambda g, c=chunk: (g, c, 0))
        update_start, normed = pl.pallas_call(
            functools.partial(start_kernel, row_size),
            grid=(rows // group,),
            in_specs=[pair_block]
            + [pl.BlockSpec((group, packed, width), lambda g: (g, 0, 0))] * row_size
            + [
                whole(start_gain),
                whole(start_head_gain),
                whole(start_in),
                whole(start_out),
                whole(end_gain),
            ]
            + [anywhere] * len(extra),
            out_specs=[pair_block, pl.BlockSpec((group, part, width), lambda g: (g, 0, 0))],
            out_shape=[full, jax.ShapeDtypeStruct((rows, part, width), BF16)],
            input_output_aliases={6 + row_size: 0} if extra else {},
            compiler_params=params(),
            cost_estimate=cost(1e10),
            name="start_finish",
        )(
            pair,
            *row_states,
            advance(start_gain),
            start_head_gain,
            start_in,
            start_out,
            end_gain,
            *extra,
        )
        normed_parts.append(normed)
        state = pl.pallas_call(
            functools.partial(column_state_kernel, chunk * part),
            grid=(tiles,),
            in_specs=[
                smem,
                pl.BlockSpec((rows, tile, width), lambda g: (0, g, 0)),
                whole(row_mask),
                whole(end_in),
            ],
            out_specs=pl.BlockSpec((1, block, width), lambda g: (g, 0, 0)),
            out_shape=jax.ShapeDtypeStruct((tiles, block, width), BF16),
            scratch_shapes=[pltpu.VMEM((rows * tile, width), F32)],
            compiler_params=params(),
            cost_estimate=cost(6e9),
            name="column_state",
        )(col_valid, normed, advance(row_mask), end_in)
        order = bits if chunk % 2 == 0 else bits[1:] + bits[:1]
        state = jnp.pad(state.reshape(tiles * block, width), ((0, pad), (0, 0)))
        column_states.append([])
        flying.append(exchange_sum(state, size, order, column_states[-1]))

    outs = []
    pieces = [(tiles + 1) // 2, tiles // 2]
    for chunk in range(chunks):
        done = 0
        for piece in pieces:
            if not piece:
                continue
            small = advance(end_head_gain)
            while not column_states[chunk]:
                small = advance(small)
            state = column_states[chunk][0][: tiles * block].reshape(tiles, block, width)
            pair_block = pl.BlockSpec(
                (rows, tile, width), lambda g, c=chunk * tiles + done: (0, c + g, 0)
            )
            outs = pl.pallas_call(
                end_kernel,
                grid=(piece,),
                in_specs=[
                    pl.BlockSpec((rows, tile, width), lambda g, c=done: (0, c + g, 0)),
                    pair_block,
                    pair_block,
                    pl.BlockSpec((1, block, width), lambda g, c=done: (c + g, 0, 0)),
                    whole(end_head_gain),
                    whole(end_in),
                    whole(end_out),
                    whole(trans_gain),
                    whole(trans_in),
                    whole(trans_out),
                ]
                + [anywhere] * len(outs),
                out_specs=[pair_block, pair_block],
                out_shape=[full, full],
                scratch_shapes=[pltpu.VMEM((rows * tile, width), F32)] * 2,
                input_output_aliases={10: 0, 11: 1} if outs else {},
                compiler_params=params(),
                cost_estimate=cost(1e10),
                name="end_finish",
            )(
                normed_parts[chunk],
                pair,
                update_start,
                state,
                small,
                end_in,
                end_out,
                trans_gain,
                trans_in,
                trans_out,
                *outs,
            )
            done += piece
    return (update_start, outs[0], outs[1])


def solution(mesh):
    field = P(("groups", "col"), "row", None)
    in_specs = (field, P("groups")) + (P(),) * 11
    return jax.shard_map(
        functools.partial(shards, mesh.shape["col"], mesh.shape["row"]),
        mesh=mesh,
        in_specs=in_specs,
        out_specs=(field, field, field),
        check_vma=False,
    )
```

```python
import functools
import math

import jax
import jax.numpy as jnp
from jax import lax
from jax.experimental import pallas as pl
from jax.experimental.pallas import tpu as pltpu
from jax.sharding import PartitionSpec as P

HEADS = 4
EPSILON = 1e-05
F32 = jnp.float32
BF16 = jnp.bfloat16
CHUNKS = 4
VMEM_BYTES = 52 * 1024 * 1024


def mean_matrix(width):
    return jnp.full((width, width), 1.0 / width, BF16)


def center_matrix(width, copies):
    rows = lax.broadcasted_iota(jnp.int32, (width, width), 0)
    cols = lax.broadcasted_iota(jnp.int32, (width, width), 1)
    once = jnp.where(rows == cols, 1.0 - 1.0 / width, -1.0 / width)
    return jnp.concatenate([once] * copies, axis=0).astype(BF16)


def layer_norm(parts, scales):
    width = parts[0].shape[-1]
    joined = parts[0] if len(parts) == 1 else jnp.concatenate(parts, axis=1)
    centered = matmul(joined, center_matrix(width, len(parts)))
    variance = matmul((centered * centered).astype(BF16), mean_matrix(width))
    return (centered * lax.rsqrt(variance + EPSILON) * scales).astype(BF16)


def feature(values):
    return jnp.maximum(values + 1.0, jnp.exp(jnp.minimum(values, 0.0)))


def sigmoid(values):
    return 0.5 + 0.5 * jnp.tanh(0.5 * values)


def matmul(left, right):
    return jnp.dot(left, right, preferred_element_type=F32)


def same_head(width):
    depth = width // HEADS
    rows = lax.broadcasted_iota(jnp.int32, (width, width), 0) // depth
    cols = lax.broadcasted_iota(jnp.int32, (width, width), 1) // depth
    return rows == cols


def outer_compact(keys, values):
    width = keys.shape[-1]
    depth = width // HEADS
    full = lax.dot_general(keys, values, (((0,), (0,)), ((), ())), preferred_element_type=F32)
    head = lax.broadcasted_iota(jnp.int32, (depth, width), 1) // depth
    result = full[:depth]
    for h in range(1, HEADS):
        result = jnp.where(head == h, full[h * depth : (h + 1) * depth], result)
    return result


def expand(state, same):
    tiled = jnp.concatenate([state.astype(F32)] * HEADS, axis=0)
    return jnp.where(same, tiled, 0.0).astype(BF16)


def query_gate(w):
    width = w.shape[0]
    return jnp.concatenate([w[:, :width], w[:, 3 * width :]], axis=1)


def head_norm(numer, denom, gate, head_gain):
    attended = numer * pl.reciprocal(jnp.maximum(denom, 1.0))
    square = matmul((attended * attended).astype(BF16), mean_matrix(numer.shape[-1]))
    scale = lax.rsqrt(square + EPSILON)
    return (attended * scale * head_gain * sigmoid(gate)).astype(BF16)


def row_state_kernel(row_valid, pair, col_mask, gain, w, out):
    count, cols, width = pair.shape
    depth = width // HEADS
    base = pl.program_id(0) * count
    normed = layer_norm([pair[...].reshape(count * cols, width)], gain[...])
    project = matmul(normed, w[:, width : 3 * width])
    keys = feature(project[:, :width]).reshape(count, cols, width) * col_mask[...][None]
    keys = keys.astype(BF16)
    values = project[:, width:].reshape(count, cols, width).astype(BF16)
    for i in range(count):
        valid = row_valid[base + i]
        out[i, 0:depth, :] = (outer_compact(keys[i], values[i]) * valid).astype(BF16)
        total = jnp.sum(keys[i].astype(F32), axis=0, keepdims=True) * valid
        out[i, depth : depth + 16, :] = jnp.broadcast_to(total, (16, width)).astype(BF16)


def start_kernel(row_size, pair, *rest):
    states, rest = rest[:row_size], rest[row_size:]
    gain, head_gain, w, w_out, end_gain = rest[:5]
    update, normed_end = rest[-2:]
    count, cols, width = pair.shape
    depth = width // HEADS
    same = same_head(width)
    ones = same.astype(F32).astype(BF16)
    field = pair[...].reshape(count * cols, width)
    project = matmul(layer_norm([field], gain[...]), query_gate(w[...]))
    queries = feature(project[:, :width]).reshape(count, cols, width).astype(BF16)
    numer, weighted = [], []
    for i in range(count):
        state = sum(s[i, 0:depth, :].astype(F32) for s in states)
        totals = sum(s[i, depth : depth + 16, :].astype(F32) for s in states)
        numer.append(matmul(queries[i], expand(state, same)))
        weighted.append(queries[i].astype(F32) * totals[0:1])
    denom = matmul(jnp.concatenate(weighted, axis=0).astype(BF16), ones)
    scaled = head_norm(
        jnp.concatenate(numer, axis=0), denom, project[:, width:], head_gain[...]
    )
    result = matmul(scaled, w_out[...]).astype(BF16)
    update[...] = result.reshape(count, cols, width)
    normed_end[...] = layer_norm([field, result], end_gain[...]).reshape(count, cols, width)


def columns_first(normed, scratch):
    rows, count, width = normed.shape
    scratch[...] = normed[...].astype(F32).reshape(rows * count, width)
    return jnp.concatenate(
        [scratch[pl.ds(j, rows, stride=count), :] for j in range(count)], axis=0
    ).astype(BF16)


def column_state_kernel(first, col_valid, normed, row_mask, w, out, scratch):
    rows, count, width = normed.shape
    depth = width // HEADS
    base = first + pl.program_id(0) * count
    project = matmul(columns_first(normed, scratch), w[:, width : 3 * width])
    keys = feature(project[:, :width]).reshape(count, rows, width) * row_mask[...][None]
    keys = keys.astype(BF16)
    values = project[:, width:].reshape(count, rows, width).astype(BF16)
    totals = []
    for j in range(count):
        valid = col_valid[base + j]
        out[0, j * depth : (j + 1) * depth, :] = (
            outer_compact(keys[j], values[j]) * valid
        ).astype(BF16)
        totals.append(jnp.sum(keys[j].astype(F32), axis=0, keepdims=True) * valid)
    out[0, count * depth : count * (depth + 1), :] = jnp.concatenate(totals, axis=0).astype(BF16)


def end_kernel(
    normed, pair, update_start, state, head_gain, w, w_out, trans_gain, trans_in, trans_out, *rest
):
    update_end, update_trans, scratch, turned = rest[-4:]
    rows, count, width = normed.shape
    depth = width // HEADS
    hidden = trans_out.shape[0]
    same = same_head(width)
    ones = same.astype(F32).astype(BF16)
    project = matmul(columns_first(normed, scratch), query_gate(w[...]))
    queries = feature(project[:, :width]).reshape(count, rows, width).astype(BF16)
    totals = state[0, count * depth : count * (depth + 1), :].astype(F32)
    numer, weighted = [], []
    for j in range(count):
        numer.append(matmul(queries[j], expand(state[0, j * depth : (j + 1) * depth, :], same)))
        weighted.append(queries[j].astype(F32) * totals[j : j + 1])
    denom = matmul(jnp.concatenate(weighted, axis=0).astype(BF16), ones)
    scaled = head_norm(
        jnp.concatenate(numer, axis=0), denom, project[:, width:], head_gain[...]
    )
    result = matmul(scaled, w_out[...])
    for j in range(count):
        turned[pl.ds(j, rows, stride=count), :] = result[j * rows : (j + 1) * rows]
    ended = turned[...].astype(BF16)
    update_end[...] = ended.reshape(rows, count, width)
    parts = [part[...].reshape(rows * count, width) for part in (pair, update_start)]
    y = layer_norm(parts + [ended], trans_gain[...])
    step = math.gcd(hidden, 256)
    moved = jnp.zeros((rows * count, width), F32)
    for at in range(0, hidden, step):
        gate = (0.5 * matmul(y, trans_in[:, at : at + step])).astype(BF16)
        up = matmul(y, trans_in[:, hidden + at : hidden + at + step]).astype(BF16)
        h = (gate + gate * jnp.tanh(gate)) * up
        moved = moved + matmul(h, trans_out[at : at + step, :])
    update_trans[...] = moved.astype(BF16).reshape(rows, count, width)


def exchange_sum(values, size, bits, done):
    me = lax.axis_index("col")
    for bit in bits:
        yield values
        half = values.shape[0] // 2
        mine = (me >> bit) & 1
        pairs = [(d, d ^ (1 << bit)) for d in range(size)]
        sent = lax.dynamic_slice_in_dim(values, (1 - mine) * half, half)
        kept = lax.dynamic_slice_in_dim(values, mine * half, half)
        got = lax.ppermute(sent, "col", pairs)
        values = (kept.astype(F32) + got.astype(F32)).astype(BF16)
    for bit in reversed(bits):
        yield values
        mine = (me >> bit) & 1
        pairs = [(d, d ^ (1 << bit)) for d in range(size)]
        got = lax.ppermute(values, "col", pairs)
        values = jnp.where(
            mine == 1,
            jnp.concatenate([got, values], axis=0),
            jnp.concatenate([values, got], axis=0),
        )
    done.append(values)


def params():
    return pltpu.CompilerParams(vmem_limit_bytes=VMEM_BYTES, dimension_semantics=("arbitrary",))


def cost(flops):
    return pl.CostEstimate(flops=int(flops), bytes_accessed=1 << 20, transcendentals=0)


def shards(
    size,
    row_size,
    pair,
    token_mask,
    start_gain,
    start_head_gain,
    start_in,
    start_out,
    end_gain,
    end_head_gain,
    end_in,
    end_out,
    trans_gain,
    trans_in,
    trans_out,
):
    rows, cols, width = pair.shape
    depth = width // HEADS
    valid = token_mask.astype(F32)
    row_valid = lax.dynamic_slice_in_dim(valid, lax.axis_index("col") * rows, rows)
    col_valid = lax.dynamic_slice_in_dim(valid, lax.axis_index("row") * cols, cols)
    row_mask = jnp.broadcast_to(row_valid[:, None], (rows, width))
    col_mask = jnp.broadcast_to(col_valid[:, None], (cols, width))
    gains = [
        g.reshape(1, width) for g in (start_gain, start_head_gain, end_gain, end_head_gain, trans_gain)
    ]
    start_gain, start_head_gain, end_gain, end_head_gain, trans_gain = gains
    smem = pl.BlockSpec(memory_space=pltpu.SMEM)
    anywhere = pl.BlockSpec(memory_space=pl.ANY)

    def whole(array):
        return pl.BlockSpec(array.shape, lambda g: (0,) * array.ndim)

    group = math.gcd(rows, 8)
    packed = depth + 16
    row_state = pl.pallas_call(
        row_state_kernel,
        grid=(rows // group,),
        in_specs=[
            smem,
            pl.BlockSpec((group, cols, width), lambda g: (g, 0, 0)),
            whole(col_mask),
            whole(start_gain),
            whole(start_in),
        ],
        out_specs=pl.BlockSpec((group, packed, width), lambda g: (g, 0, 0)),
        out_shape=jax.ShapeDtypeStruct((rows, packed, width), BF16),
        compiler_params=params(),
        cost_estimate=cost(2e10),
        name="row_state",
    )(row_valid, pair, col_mask, start_gain, start_in)
    row_states = [row_state] + [
        lax.ppermute(row_state, "row", [(d, (d + k) % row_size) for d in range(row_size)])
        for k in range(1, row_size)
    ]

    tile = 16
    chunks = math.gcd(cols // tile, CHUNKS)
    part = cols // chunks
    tiles = part // tile
    block = tile * (depth + 1)
    pad = -(tiles * block) % (16 * size)
    bits = list(range(size.bit_length() - 1))
    full = jax.ShapeDtypeStruct(pair.shape, BF16)
    flying = []

    def advance(small):
        for steps in list(flying):
            ready = next(steps, None)
            if ready is None:
                flying.remove(steps)
            else:
                small, _ = lax.optimization_barrier((small, ready))
        return small

    group = math.gcd(rows, 16)
    update_start = None
    normed_parts, column_states = [], []
    for chunk in range(chunks):
        extra = [] if update_start is None else [update_start]
        pair_block = pl.BlockSpec((group, part, width), lambda g, c=chunk: (g, c, 0))
        update_start, normed = pl.pallas_call(
            functools.partial(start_kernel, row_size),
            grid=(rows // group,),
            in_specs=[pair_block]
            + [pl.BlockSpec((group, packed, width), lambda g: (g, 0, 0))] * row_size
            + [
                whole(start_gain),
                whole(start_head_gain),
                whole(start_in),
                whole(start_out),
                whole(end_gain),
            ]
            + [anywhere] * len(extra),
            out_specs=[pair_block, pl.BlockSpec((group, part, width), lambda g: (g, 0, 0))],
            out_shape=[full, jax.ShapeDtypeStruct((rows, part, width), BF16)],
            input_output_aliases={6 + row_size: 0} if extra else {},
            compiler_params=params(),
            cost_estimate=cost(1e10),
            name="start_finish",
        )(
            pair,
            *row_states,
            advance(start_gain),
            start_head_gain,
            start_in,
            start_out,
            end_gain,
            *extra,
        )
        normed_parts.append(normed)
        state = pl.pallas_call(
            functools.partial(column_state_kernel, chunk * part),
            grid=(tiles,),
            in_specs=[
                smem,
                pl.BlockSpec((rows, tile, width), lambda g: (0, g, 0)),
                whole(row_mask),
                whole(end_in),
            ],
            out_specs=pl.BlockSpec((1, block, width), lambda g: (g, 0, 0)),
            out_shape=jax.ShapeDtypeStruct((tiles, block, width), BF16),
            scratch_shapes=[pltpu.VMEM((rows * tile, width), F32)],
            compiler_params=params(),
            cost_estimate=cost(6e9),
            name="column_state",
        )(col_valid, normed, advance(row_mask), end_in)
        order = bits if chunk % 2 == 0 else bits[1:] + bits[:1]
        state = jnp.pad(state.reshape(tiles * block, width), ((0, pad), (0, 0)))
        column_states.append([])
        flying.append(exchange_sum(state, size, order, column_states[-1]))

    outs = []
    for chunk in range(chunks):
        done = 0
        pieces = [(tiles + 1) // 2, tiles // 2] if 2 * chunk < chunks else [tiles]
        for piece in pieces:
            if not piece:
                continue
            small = advance(end_head_gain)
            while not column_states[chunk]:
                small = advance(small)
            state = column_states[chunk][0][: tiles * block].reshape(tiles, block, width)
            pair_block = pl.BlockSpec(
                (rows, tile, width), lambda g, c=chunk * tiles + done: (0, c + g, 0)
            )
            outs = pl.pallas_call(
                end_kernel,
                grid=(piece,),
                in_specs=[
                    pl.BlockSpec((rows, tile, width), lambda g, c=done: (0, c + g, 0)),
                    pair_block,
                    pair_block,
                    pl.BlockSpec((1, block, width), lambda g, c=done: (c + g, 0, 0)),
                    whole(end_head_gain),
                    whole(end_in),
                    whole(end_out),
                    whole(trans_gain),
                    whole(trans_in),
                    whole(trans_out),
                ]
                + [anywhere] * len(outs),
                out_specs=[pair_block, pair_block],
                out_shape=[full, full],
                scratch_shapes=[pltpu.VMEM((rows * tile, width), F32)] * 2,
                input_output_aliases={10: 0, 11: 1} if outs else {},
                compiler_params=params(),
                cost_estimate=cost(1e10),
                name="end_finish",
            )(
                normed_parts[chunk],
                pair,
                update_start,
                state,
                small,
                end_in,
                end_out,
                trans_gain,
                trans_in,
                trans_out,
                *outs,
            )
            done += piece
    return (update_start, outs[0], outs[1])


def solution(mesh):
    field = P(("groups", "col"), "row", None)
    in_specs = (field, P("groups")) + (P(),) * 11
    return jax.shard_map(
        functools.partial(shards, mesh.shape["col"], mesh.shape["row"]),
        mesh=mesh,
        in_specs=in_specs,
        out_specs=(field, field, field),
        check_vma=False,
    )
```

```python
import functools
import math

import jax
import jax.numpy as jnp
from jax import lax
from jax.experimental import pallas as pl
from jax.experimental.pallas import tpu as pltpu
from jax.sharding import PartitionSpec as P

HEADS = 4
EPSILON = 1e-05
F32 = jnp.float32
BF16 = jnp.bfloat16
CHUNKS = 4
VMEM_BYTES = 52 * 1024 * 1024


def mean_matrix(width):
    return jnp.full((width, width), 1.0 / width, BF16)


def center_matrix(width, copies):
    rows = lax.broadcasted_iota(jnp.int32, (width, width), 0)
    cols = lax.broadcasted_iota(jnp.int32, (width, width), 1)
    once = jnp.where(rows == cols, 1.0 - 1.0 / width, -1.0 / width)
    return jnp.concatenate([once] * copies, axis=0).astype(BF16)


def layer_norm(parts, scales):
    width = parts[0].shape[-1]
    joined = parts[0] if len(parts) == 1 else jnp.concatenate(parts, axis=1)
    centered = matmul(joined, center_matrix(width, len(parts)))
    variance = matmul((centered * centered).astype(BF16), mean_matrix(width))
    return (centered * lax.rsqrt(variance + EPSILON) * scales).astype(BF16)


def feature(values):
    return jnp.maximum(values + 1.0, jnp.exp(jnp.minimum(values, 0.0)))


def sigmoid(values):
    return 0.5 + 0.5 * jnp.tanh(0.5 * values)


def matmul(left, right):
    return jnp.dot(left, right, preferred_element_type=F32)


def same_head(width):
    depth = width // HEADS
    rows = lax.broadcasted_iota(jnp.int32, (width, width), 0) // depth
    cols = lax.broadcasted_iota(jnp.int32, (width, width), 1) // depth
    return rows == cols


def outer_compact(keys, values):
    width = keys.shape[-1]
    depth = width // HEADS
    full = lax.dot_general(keys, values, (((0,), (0,)), ((), ())), preferred_element_type=F32)
    head = lax.broadcasted_iota(jnp.int32, (depth, width), 1) // depth
    result = full[:depth]
    for h in range(1, HEADS):
        result = jnp.where(head == h, full[h * depth : (h + 1) * depth], result)
    return result


def expand(state, same):
    tiled = jnp.concatenate([state.astype(F32)] * HEADS, axis=0)
    return jnp.where(same, tiled, 0.0).astype(BF16)


def query_gate(w):
    width = w.shape[0]
    return jnp.concatenate([w[:, :width], w[:, 3 * width :]], axis=1)


def head_norm(numer, denom, gate, head_gain):
    attended = numer * pl.reciprocal(jnp.maximum(denom, 1.0))
    square = matmul((attended * attended).astype(BF16), mean_matrix(numer.shape[-1]))
    scale = lax.rsqrt(square + EPSILON)
    return (attended * scale * head_gain * sigmoid(gate.astype(BF16)).astype(F32)).astype(BF16)


def row_state_kernel(row_valid, pair, col_mask, gain, w, out):
    count, cols, width = pair.shape
    depth = width // HEADS
    base = pl.program_id(0) * count
    normed = layer_norm([pair[...].reshape(count * cols, width)], gain[...])
    project = matmul(normed, w[:, width : 3 * width])
    keys = feature(project[:, :width].astype(BF16)).reshape(count, cols, width) * col_mask[...].astype(BF16)[None]
    values = project[:, width:].reshape(count, cols, width).astype(BF16)
    for i in range(count):
        valid = row_valid[base + i]
        out[i, 0:depth, :] = (outer_compact(keys[i], values[i]) * valid).astype(BF16)
        total = jnp.sum(keys[i].astype(F32), axis=0, keepdims=True) * valid
        out[i, depth : depth + 16, :] = jnp.broadcast_to(total, (16, width)).astype(BF16)


def start_kernel(row_size, pair, *rest):
    states, rest = rest[:row_size], rest[row_size:]
    gain, head_gain, w, w_out, end_gain = rest[:5]
    update, normed_end = rest[-2:]
    count, cols, width = pair.shape
    depth = width // HEADS
    same = same_head(width)
    ones = same.astype(F32).astype(BF16)
    field = pair[...].reshape(count * cols, width)
    project = matmul(layer_norm([field], gain[...]), query_gate(w[...]))
    queries = feature(project[:, :width].astype(BF16)).reshape(count, cols, width).astype(BF16)
    numer, weighted = [], []
    for i in range(count):
        state = sum(s[i, 0:depth, :].astype(F32) for s in states)
        totals = sum(s[i, depth : depth + 16, :].astype(F32) for s in states)
        numer.append(matmul(queries[i], expand(state, same)))
        weighted.append(queries[i].astype(F32) * totals[0:1])
    denom = matmul(jnp.concatenate(weighted, axis=0).astype(BF16), ones)
    scaled = head_norm(
        jnp.concatenate(numer, axis=0), denom, project[:, width:], head_gain[...]
    )
    result = matmul(scaled, w_out[...]).astype(BF16)
    update[...] = result.reshape(count, cols, width)
    normed_end[...] = layer_norm([field, result], end_gain[...]).reshape(count, cols, width)


def columns_first(normed, scratch):
    rows, count, width = normed.shape
    scratch[...] = normed[...].astype(F32).reshape(rows * count, width)
    return jnp.concatenate(
        [scratch[pl.ds(j, rows, stride=count), :] for j in range(count)], axis=0
    ).astype(BF16)


def column_state_kernel(first, col_valid, normed, row_mask, w, out, scratch):
    rows, count, width = normed.shape
    depth = width // HEADS
    base = first + pl.program_id(0) * count
    project = matmul(columns_first(normed, scratch), w[:, width : 3 * width])
    keys = feature(project[:, :width].astype(BF16)).reshape(count, rows, width) * row_mask[...].astype(BF16)[None]
    values = project[:, width:].reshape(count, rows, width).astype(BF16)
    totals = []
    for j in range(count):
        valid = col_valid[base + j]
        out[0, j * depth : (j + 1) * depth, :] = (
            outer_compact(keys[j], values[j]) * valid
        ).astype(BF16)
        totals.append(jnp.sum(keys[j].astype(F32), axis=0, keepdims=True) * valid)
    out[0, count * depth : count * (depth + 1), :] = jnp.concatenate(totals, axis=0).astype(BF16)


def end_kernel(
    normed, pair, update_start, state, head_gain, w, w_out, trans_gain, trans_in, trans_out, *rest
):
    update_end, update_trans, scratch, turned = rest[-4:]
    rows, count, width = normed.shape
    depth = width // HEADS
    hidden = trans_out.shape[0]
    same = same_head(width)
    ones = same.astype(F32).astype(BF16)
    project = matmul(columns_first(normed, scratch), query_gate(w[...]))
    queries = feature(project[:, :width].astype(BF16)).reshape(count, rows, width).astype(BF16)
    totals = state[0, count * depth : count * (depth + 1), :].astype(F32)
    numer, weighted = [], []
    for j in range(count):
        numer.append(matmul(queries[j], expand(state[0, j * depth : (j + 1) * depth, :], same)))
        weighted.append(queries[j].astype(F32) * totals[j : j + 1])
    denom = matmul(jnp.concatenate(weighted, axis=0).astype(BF16), ones)
    scaled = head_norm(
        jnp.concatenate(numer, axis=0), denom, project[:, width:], head_gain[...]
    )
    result = matmul(scaled, w_out[...])
    for j in range(count):
        turned[pl.ds(j, rows, stride=count), :] = result[j * rows : (j + 1) * rows]
    ended = turned[...].astype(BF16)
    update_end[...] = ended.reshape(rows, count, width)
    parts = [part[...].reshape(rows * count, width) for part in (pair, update_start)]
    y = layer_norm(parts + [ended], trans_gain[...])
    step = math.gcd(hidden, 256)
    moved = jnp.zeros((rows * count, width), F32)
    for at in range(0, hidden, step):
        gate = (0.5 * matmul(y, trans_in[:, at : at + step])).astype(BF16)
        up = matmul(y, trans_in[:, hidden + at : hidden + at + step]).astype(BF16)
        h = (gate + gate * jnp.tanh(gate)) * up
        moved = moved + matmul(h, trans_out[at : at + step, :])
    update_trans[...] = moved.astype(BF16).reshape(rows, count, width)


def exchange_sum(values, size, bits, done, last):
    def after(got):
        return lax.optimization_barrier((got, last[-1]))[0] if last else got

    me = lax.axis_index("col")
    for bit in bits:
        half = values.shape[0] // 2
        mine = (me >> bit) & 1
        pairs = [(d, d ^ (1 << bit)) for d in range(size)]
        sent = lax.dynamic_slice_in_dim(values, (1 - mine) * half, half)
        kept = lax.dynamic_slice_in_dim(values, mine * half, half)
        got = lax.ppermute(sent, "col", pairs)
        yield values
        got = after(got)
        values = (kept.astype(F32) + got.astype(F32)).astype(BF16)
    for bit in reversed(bits):
        mine = (me >> bit) & 1
        pairs = [(d, d ^ (1 << bit)) for d in range(size)]
        got = lax.ppermute(values, "col", pairs)
        yield values
        got = after(got)
        values = jnp.where(
            mine == 1,
            jnp.concatenate([got, values], axis=0),
            jnp.concatenate([values, got], axis=0),
        )
    done.append(values)


def params():
    return pltpu.CompilerParams(vmem_limit_bytes=VMEM_BYTES, dimension_semantics=("arbitrary",))


def cost(flops):
    return pl.CostEstimate(flops=int(flops), bytes_accessed=1 << 20, transcendentals=0)


def shards(
    size,
    row_size,
    pair,
    token_mask,
    start_gain,
    start_head_gain,
    start_in,
    start_out,
    end_gain,
    end_head_gain,
    end_in,
    end_out,
    trans_gain,
    trans_in,
    trans_out,
):
    rows, cols, width = pair.shape
    depth = width // HEADS
    valid = token_mask.astype(F32)
    row_valid = lax.dynamic_slice_in_dim(valid, lax.axis_index("col") * rows, rows)
    col_valid = lax.dynamic_slice_in_dim(valid, lax.axis_index("row") * cols, cols)
    row_mask = jnp.broadcast_to(row_valid[:, None], (rows, width))
    col_mask = jnp.broadcast_to(col_valid[:, None], (cols, width))
    gains = [
        g.reshape(1, width) for g in (start_gain, start_head_gain, end_gain, end_head_gain, trans_gain)
    ]
    start_gain, start_head_gain, end_gain, end_head_gain, trans_gain = gains
    smem = pl.BlockSpec(memory_space=pltpu.SMEM)
    anywhere = pl.BlockSpec(memory_space=pl.ANY)

    def whole(array):
        return pl.BlockSpec(array.shape, lambda g: (0,) * array.ndim)

    group = math.gcd(rows, 8)
    packed = depth + 16
    row_state = pl.pallas_call(
        row_state_kernel,
        grid=(rows // group,),
        in_specs=[
            smem,
            pl.BlockSpec((group, cols, width), lambda g: (g, 0, 0)),
            whole(col_mask),
            whole(start_gain),
            whole(start_in),
        ],
        out_specs=pl.BlockSpec((group, packed, width), lambda g: (g, 0, 0)),
        out_shape=jax.ShapeDtypeStruct((rows, packed, width), BF16),
        compiler_params=params(),
        cost_estimate=cost(2e10),
        name="row_state",
    )(row_valid, pair, col_mask, start_gain, start_in)
    row_states = [row_state] + [
        lax.ppermute(row_state, "row", [(d, (d + k) % row_size) for d in range(row_size)])
        for k in range(1, row_size)
    ]

    tile = 16
    chunks = math.gcd(cols // tile, CHUNKS)
    part = cols // chunks
    tiles = part // tile
    block = tile * (depth + 1)
    pad = -(tiles * block) % (16 * size)
    bits = list(range(size.bit_length() - 1))
    full = jax.ShapeDtypeStruct(pair.shape, BF16)
    flying, last = [], []

    def advance(small):
        for steps in list(flying):
            ready = next(steps, None)
            if ready is None:
                flying.remove(steps)
            else:
                small, _ = lax.optimization_barrier((small, ready))
        return small

    group = math.gcd(rows, 16)
    update_start = None
    normed_parts, column_states = [], []
    for chunk in range(chunks):
        extra = [] if update_start is None else [update_start]
        pair_block = pl.BlockSpec((group, part, width), lambda g, c=chunk: (g, c, 0))
        update_start, normed = pl.pallas_call(
            functools.partial(start_kernel, row_size),
            grid=(rows // group,),
            in_specs=[pair_block]
            + [pl.BlockSpec((group, packed, width), lambda g: (g, 0, 0))] * row_size
            + [
                whole(start_gain),
                whole(start_head_gain),
                whole(start_in),
                whole(start_out),
                whole(end_gain),
            ]
            + [anywhere] * len(extra),
            out_specs=[pair_block, pl.BlockSpec((group, part, width), lambda g: (g, 0, 0))],
            out_shape=[full, jax.ShapeDtypeStruct((rows, part, width), BF16)],
            input_output_aliases={6 + row_size: 0} if extra else {},
            compiler_params=params(),
            cost_estimate=cost(1e10),
            name="start_finish",
        )(
            pair,
            *row_states,
            advance(start_gain),
            start_head_gain,
            start_in,
            start_out,
            end_gain,
            *extra,
        )
        normed_parts.append(normed)
        last[:] = [normed]
        state = pl.pallas_call(
            functools.partial(column_state_kernel, chunk * part),
            grid=(tiles,),
            in_specs=[
                smem,
                pl.BlockSpec((rows, tile, width), lambda g: (0, g, 0)),
                whole(row_mask),
                whole(end_in),
            ],
            out_specs=pl.BlockSpec((1, block, width), lambda g: (g, 0, 0)),
            out_shape=jax.ShapeDtypeStruct((tiles, block, width), BF16),
            scratch_shapes=[pltpu.VMEM((rows * tile, width), F32)],
            compiler_params=params(),
            cost_estimate=cost(6e9),
            name="column_state",
        )(col_valid, normed, advance(row_mask), end_in)
        order = bits if chunk % 2 == 0 else bits[1:] + bits[:1]
        last[:] = [state]
        state = jnp.pad(state.reshape(tiles * block, width), ((0, pad), (0, 0)))
        column_states.append([])
        flying.append(exchange_sum(state, size, order, column_states[-1], last))

    outs = []
    for chunk in range(chunks):
        last[:] = []
        done = 0
        pieces = [(tiles + 1) // 2, tiles // 2] if 2 * chunk < chunks else [tiles]
        for piece in pieces:
            if not piece:
                continue
            small = advance(end_head_gain)
            while not column_states[chunk]:
                small = advance(small)
            state = column_states[chunk][0][: tiles * block].reshape(tiles, block, width)
            pair_block = pl.BlockSpec(
                (rows, tile, width), lambda g, c=chunk * tiles + done: (0, c + g, 0)
            )
            outs = pl.pallas_call(
                end_kernel,
                grid=(piece,),
                in_specs=[
                    pl.BlockSpec((rows, tile, width), lambda g, c=done: (0, c + g, 0)),
                    pair_block,
                    pair_block,
                    pl.BlockSpec((1, block, width), lambda g, c=done: (c + g, 0, 0)),
                    whole(end_head_gain),
                    whole(end_in),
                    whole(end_out),
                    whole(trans_gain),
                    whole(trans_in),
                    whole(trans_out),
                ]
                + [anywhere] * len(outs),
                out_specs=[pair_block, pair_block],
                out_shape=[full, full],
                scratch_shapes=[pltpu.VMEM((rows * tile, width), F32)] * 2,
                input_output_aliases={10: 0, 11: 1} if outs else {},
                compiler_params=params(),
                cost_estimate=cost(1e10),
                name="end_finish",
            )(
                normed_parts[chunk],
                pair,
                update_start,
                state,
                small,
                end_in,
                end_out,
                trans_gain,
                trans_in,
                trans_out,
                *outs,
            )
            done += piece
    return (update_start, outs[0], outs[1])


def solution(mesh):
    field = P(("groups", "col"), "row", None)
    in_specs = (field, P("groups")) + (P(),) * 11
    return jax.shard_map(
        functools.partial(shards, mesh.shape["col"], mesh.shape["row"]),
        mesh=mesh,
        in_specs=in_specs,
        out_specs=(field, field, field),
        check_vma=False,
    )
```
